128 devices in a mesh: outer: 16 (over z, y_lo, core), inner: 8 (over x, y_hi).
Axes of the slice: x: 4, y: 4 (y_hi: 2, y_lo: 2; y = y_hi * 2 + y_lo), z: 4, core: 2. Of those that a mesh axis runs over, the one named last changes fastest.
Arguments:
- params: bfloat16 [8, 1536, 512], P('inner', 'outer'), may hold values from -0.0546875 to 0.0546875
- moment: bfloat16 [8, 1536, 512], P('inner', 'outer'), may hold values from -6 to 6
- second: bfloat16 [8, 1536, 512], P('inner', 'outer'), may hold values from 0.0099487305 to 4
- grad_prev: float32 [8, 1536, 512], P('inner', 'outer'), may hold values from -6 to 6
- tokens: bfloat16 [49152, 12288], P(('outer', 'inner')), may hold values from -24 to 24
- cotangent: bfloat16 [49152, 12288], P(('outer', 'inner')), may hold values from -0.109375 to 0.109375
Outputs:
- fresh: bfloat16 [8, 1536, 512], P('inner', 'outer')
- moment_new: bfloat16 [8, 1536, 512], P('inner', 'outer')
- second_new: bfloat16 [8, 1536, 512], P('inner', 'outer')
- gradient: float32 [8, 1536, 512], P('inner', 'outer')
The draws below stay inside these ranges and needn't reach their ends.
All inputs are finite; a program needn't handle non-finite values.
Results may differ from the reference program's by a relative error of at most 0.0054.
Values may be sent and summed in bfloat16 or wider, within the bound.
A program may use at most 192 MiB of HBM per device.

```python
import math
import jax
import jax.numpy as jnp
from jax import lax

D = 12288
K = 256
TOKENS = 49152
N_INNER = 8


def with_spikes(values, rng, source, target, shards_of, factor):
    owner, partner = [(jnp.arange(values.shape[dim]) // (values.shape[dim] // shards_of)).reshape([-1 if axis == dim else 1 for axis in range(values.ndim)]) for dim in (source, target)]
    chosen = jax.random.permutation(rng, shards_of)[partner]
    strong = (owner == chosen) | (owner == (partner + shards_of // 2) % shards_of)
    return jnp.where(strong, factor * values, values)


def levels(key, dims, cuts, least, high):
    loudness = 1.0
    for position, blocks in cuts:
        draws = jax.random.uniform(jax.random.fold_in(jax.random.fold_in(key, 6), position), (blocks,), jnp.float32, least / len(cuts), high / len(cuts))
        loudness = loudness * jnp.repeat(jnp.exp(draws), dims[position] // blocks).reshape((-1,) + (1,) * (len(dims) - 1 - position))
    return loudness


def scatter_about(stream_key, shape, spread, reach, split=(), kind=jnp.bfloat16):
    result = jax.random.normal(stream_key, shape, jnp.float32) * spread
    if len(split) > 0:
        result = levels(stream_key, shape, split, -0.22, 0.18) * result
    return jnp.clip(result, min=-reach, max=reach).astype(kind)


def heavy_noise(own_key, extent, deviation, bound, shards, heavy, kind=jnp.bfloat16):
    array = deviation * jax.random.normal(own_key, extent, jnp.float32)
    if shards:
        array = array * levels(own_key, extent, shards, -0.22, 0.18)
    return jnp.clip(with_spikes(array, jax.random.fold_in(own_key, 3), *heavy), -bound, bound).astype(kind)


def setup_inputs(seed: int = 0) -> dict:
    streams_of = jax.random.split(jax.random.key(seed), 7)
    params = scatter_about(streams_of[0], (N_INNER, D // N_INNER, 2 * K), D ** -0.5, 0.0546875, ((0, 8), (1, 16)))
    moment = scatter_about(streams_of[1], (N_INNER, D // N_INNER, 2 * K), 1.0, 6.0, ((0, 8), (1, 16)))
    second = jnp.clip(jnp.exp(math.log(4.0) - 5.996605 * jax.random.uniform(streams_of[2], (N_INNER, D // N_INNER, 2 * K), jnp.float32) ** levels(streams_of[2], (N_INNER, D // N_INNER, 2 * K), ((0, 8), (1, 16)), -0.2, 0.2)), 0.0099487305, 4.0).astype(jnp.bfloat16)
    grad_prev = scatter_about(streams_of[3], (N_INNER, D // N_INNER, 2 * K), 1.0, 6.0, ((0, 8), (1, 16)), jnp.float32)
    tokens = heavy_noise(streams_of[4], (TOKENS, D), 1.0, 24.0, ((0, 128),), (0, 1, 128, 5.5))
    cotangent = heavy_noise(streams_of[5], (TOKENS, D), (1 / TOKENS ** 0.5), 0.109375, ((0, 128),), (0, 1, 128, 5.5))
    return {"params": params, "moment": moment, "second": second, "grad_prev": grad_prev, "tokens": tokens, "cotangent": cotangent}


beta_one = 0.9
beta_two = 0.95
bias_one = 0.9999734386011124
bias_two = 0.994079470779666
epsilon_adam = 1e-08
learn_rate = 6e-05
decay_rate = 0.1
root_scale = 0.7978845608028654
cubic_term = 0.044715

def gelu_pair(values):
    tangent = jnp.tanh(root_scale * (values + cubic_term * values * values * values))
    output = 0.5 * values * (1.0 + tangent)
    slope = 0.5 * (1.0 + tangent) + 0.5 * values * (1.0 - tangent * tangent) * root_scale * (1.0 + 3.0 * cubic_term * values * values)
    return (output, slope)

def adam_update(params, moment, second, grad_prev):
    moment_new = beta_one * moment.astype(jnp.float32) + (1.0 - beta_one) * grad_prev
    second_new = beta_two * second.astype(jnp.float32) + (1.0 - beta_two) * grad_prev * grad_prev
    update = moment_new / bias_one / (jnp.sqrt(second_new / bias_two) + epsilon_adam) + decay_rate * params.astype(jnp.float32)
    fresh = params.astype(jnp.float32) - learn_rate * update
    return (fresh.astype(jnp.bfloat16), moment_new.astype(jnp.bfloat16), second_new.astype(jnp.bfloat16))

def reference(params, moment, second, grad_prev, tokens, cotangent):
    fresh, moment_new, second_new = adam_update(params, moment, second, grad_prev)
    weights = fresh.reshape(D, 2 * K)
    preact = jnp.dot(tokens, weights[:, :K], preferred_element_type=jnp.float32)
    backward = jnp.dot(cotangent, weights[:, K:], preferred_element_type=jnp.float32)
    activ, slope = gelu_pair(preact)
    hidden = activ.astype(jnp.bfloat16)
    delta = (backward * slope).astype(jnp.bfloat16)
    contract = (((0,), (0,)), ((), ()))
    first = lax.dot_general(tokens, delta, contract, preferred_element_type=jnp.float32)
    other = lax.dot_general(cotangent, hidden, contract, preferred_element_type=jnp.float32)
    gradient = jnp.concatenate([first, other], axis=1).reshape(N_INNER, D // N_INNER, 2 * K)
    return (fresh, moment_new, second_new, gradient)
```

```python
import functools

import jax
import jax.numpy as jnp
from jax import lax
from jax.experimental import pallas as pl
from jax.experimental.pallas import tpu as pltpu
from jax.sharding import PartitionSpec as P

beta_one = 0.9
beta_two = 0.95
bias_one = 0.9999734386011124
bias_two = 0.994079470779666
epsilon_adam = 1e-08
learn_rate = 6e-05
decay_rate = 0.1
root_scale = 0.7978845608028654
cubic_term = 0.044715

MESH = pl.DeviceIdType.MESH
f32 = jnp.float32
bf16 = jnp.bfloat16

ORDER = ((0, 1, 2), (1, 2, 0), (2, 0, 1))
STEPS = (2, 1, -1, 0)
SLOT = {2: 0, 1: 1, -1: 2, 0: 3}
WAYS = (1, -1)
SIDE = {1: 0, -1: 1}


def gelu_value(values):
    tangent = jnp.tanh(root_scale * (values + cubic_term * values * values * values))
    return 0.5 * values * (1.0 + tangent)


def gelu_slope(values):
    tangent = jnp.tanh(root_scale * (values + cubic_term * values * values * values))
    return 0.5 * (1.0 + tangent) + 0.5 * values * (1.0 - tangent * tangent) * root_scale * (
        1.0 + 3.0 * cubic_term * values * values
    )


def adam_update(params, moment, second, grad_prev):
    moment_new = beta_one * moment.astype(f32) + (1.0 - beta_one) * grad_prev
    second_new = beta_two * second.astype(f32) + (1.0 - beta_two) * grad_prev * grad_prev
    update = moment_new / bias_one / (
        jnp.sqrt(second_new / bias_two) + epsilon_adam
    ) + decay_rate * params.astype(f32)
    fresh = params.astype(f32) - learn_rate * update
    return (fresh.astype(bf16), moment_new.astype(bf16), second_new.astype(bf16))


def ring(place, step):
    return lax.rem(place + (step + 4), 4)


def device(x, y, z, core):
    return {"outer": z * 4 + lax.rem(y, 2) * 2 + core, "inner": x * 2 + y // 2}


def kernel(
    params, moment, second, grad_prev, tokens, cotangent,
    fresh_out, moment_out, second_out, gradient_out,
    act, held, grads, acc, other, turned, stage,
    first_rows, full_rows, full_units, first_second, second_units, first_last, last_unit,
    final, finals, send_sems, recv_sems, local_sems,
):
    outer = lax.axis_index("outer")
    inner = lax.axis_index("inner")
    core = lax.rem(outer, 2)
    y_lo = lax.rem(outer // 2, 2)
    own = (inner // 2, lax.rem(inner, 2) * 2 + y_lo, outer // 4)

    def neighbour(axis, way):
        place = list(own)
        place[axis] = ring(place[axis], way)
        return device(*place, core)

    def partner(which):
        return device(
            own[0], own[1] - y_lo + lax.rem(y_lo + which // 2, 2), own[2], lax.rem(core + which % 2, 2)
        )

    neighbours = {(axis, way): neighbour(axis, way) for axis in range(3) for way in WAYS}
    sibling = partner(1)

    barrier = pltpu.get_barrier_semaphore()
    greeted = list(neighbours.values()) + [sibling, partner(3)]
    for one in greeted:
        pl.semaphore_signal(barrier, inc=1, device_id=one, device_id_type=MESH)

    mine = pl.ds(pl.multiple_of(core * 384, 384), 384)

    def load_own(source):
        return pltpu.make_async_copy(source, act.at[mine], local_sems.at[0])

    @pl.when(core == 0)
    def _():
        load_own(tokens).start()

    @pl.when(core == 1)
    def _():
        load_own(cotangent).start()

    messages = {}

    def send(key, source, target, to):
        index = len(messages)
        copy = pltpu.make_async_remote_copy(
            src_ref=source,
            dst_ref=target,
            send_sem=send_sems.at[index],
            recv_sem=recv_sems.at[index],
            device_id=to,
            device_id_type=MESH,
        )
        messages[key] = copy
        copy.start()

    def arrived(key):
        messages[key].wait_recv()

    fresh, moment_new, second_new = adam_update(params[0], moment[0], second[0], grad_prev[0])
    fresh_out[0] = fresh
    moment_out[0] = moment_new
    second_out[0] = second_new
    stage[0] = fresh[:, :256]
    stage[1] = fresh[:, 256:]

    pl.semaphore_wait(barrier, len(greeted))

    send("rows", stage.at[1 - core], stage.at[2], sibling)

    def load_sibling(source):
        return pltpu.make_async_remote_copy(
            src_ref=source,
            dst_ref=act.at[mine],
            send_sem=local_sems.at[1],
            recv_sem=local_sems.at[2],
            device_id=sibling,
            device_id_type=MESH,
        )

    @pl.when(core == 0)
    def _():
        load_sibling(cotangent).start()

    @pl.when(core == 1)
    def _():
        load_sibling(tokens).start()

    def places(p):
        return tuple(own[axis] for axis in ORDER[p])

    arrived("rows")
    for first_core in range(2):
        @pl.when(core == first_core)
        def _():
            low, high = (stage[first_core], stage[2]) if first_core == 0 else (stage[2], stage[first_core])
            pieces = (low[:64], jnp.concatenate([low[64:], high[:32]], axis=0), high[32:])
            for p in range(3):
                one, two, three = places(p)
                held[p, three, two, one] = pieces[p]

    def half(way, rows):
        return pl.ds(SIDE[way] * (rows // 2), rows // 2)

    def unit(p, three, two, one):
        return held.at[p, three, two, one]

    def give(key, p, level, ref):
        for way in WAYS:
            send((key[0], p, way) + key[1:], ref, ref, neighbours[ORDER[p][level], way])

    def pass_on(key, p, level, way, ref):
        send(key, ref, ref, neighbours[ORDER[p][level], way])

    for p in range(3):
        one, two, three = places(p)
        give(("g1",), p, 0, unit(p, three, two, one))
    for p in range(3):
        one, two, three = places(p)
        give(("g2", 0), p, 1, unit(p, three, two, one))
    for p in range(3):
        one, two, three = places(p)
        give(("g3", 0), p, 2, unit(p, three, two, one))
    for p in range(3):
        one, two, three = places(p)
        for way in WAYS:
            arrived(("g1", p, way))
            pass_on(("g1f", p, way), p, 0, way, held.at[p, three, two, ring(one, -way), half(way, 64)])
    for p in range(3):
        one, two, three = places(p)
        for step in WAYS:
            give(("g2", step), p, 1, unit(p, three, two, ring(one, step)))
    for p in range(3):
        one, two, three = places(p)
        for step in WAYS:
            give(("g3", step), p, 2, unit(p, three, two, ring(one, step)))

    def pass_second(p, step):
        one, two, three = places(p)
        for way in WAYS:
            arrived(("g2", p, way, step))
            pass_on(
                ("g2f", p, way, step), p, 1, way,
                held.at[p, three, ring(two, -way), ring(one, step), half(way, 64)],
            )

    for p in range(3):
        pass_second(p, 0)
    for p in range(3):
        one, two, three = places(p)
        for way in WAYS:
            arrived(("g1f", p, way))
        give(("g2", 2), p, 1, unit(p, three, two, ring(one, 2)))
        give(("g3", 2), p, 2, unit(p, three, two, ring(one, 2)))
    for p in range(3):
        for step in WAYS:
            pass_second(p, step)
    for p in range(3):
        pass_second(p, 2)
        one, two, three = places(p)
        for step in WAYS:
            give(("g3r", step), p, 2, held.at[p, three, ring(two, step)])
    for p in range(3):
        one, two, three = places(p)
        for way in WAYS:
            for step in STEPS:
                arrived(("g2f", p, way, step))
        give(("g3r", 2), p, 2, held.at[p, three, ring(two, 2)])

    def pass_third(p, step):
        one, two, three = places(p)
        for way in WAYS:
            if step == 0:
                for k in STEPS:
                    arrived(("g3", p, way, k))
            else:
                arrived(("g3r", p, way, step))
            pass_on(
                ("g3f", p, way, step), p, 2, way,
                held.at[p, ring(three, -way), ring(two, step), :, half(way, 64)],
            )

    for step in (0, 1, -1, 2):
        for p in range(3):
            pass_third(p, step)
    load_own(tokens).wait()
    load_sibling(tokens).wait()
    for step in (0, 1, -1, 2):
        for p in range(3):
            for way in WAYS:
                arrived(("g3f", p, way, step))

    def block(p, x, y, z):
        place = (x, y, z)
        return tuple(place[axis] for axis in reversed(ORDER[p]))

    def weight_rows(x, y_hi, z):
        return [
            held[(p,) + block(p, x, y_hi * 2 + low, z)] for low in range(2) for p in range(3)
        ]

    def product(step, carry):
        x, y_hi = step // 2, lax.rem(step, 2)
        rows = []
        for z in range(4):
            rows += weight_rows(x, y_hi, z)
        columns = pl.ds(pl.multiple_of(step * 1536, 1536), 1536)
        part = jnp.dot(act[:, columns], jnp.concatenate(rows, axis=0), preferred_element_type=f32)

        @pl.when(step == 0)
        def _():
            acc[...] = part

        @pl.when(step > 0)
        def _():
            acc[...] += part

        return carry

    lax.fori_loop(0, 8, product, 0)

    send("products", acc, other, sibling)
    arrived("products")
    for rows in range(3):
        span = slice(rows * 256, (rows + 1) * 256)

        @pl.when(core == 0)
        def _():
            turned[:, span] = (other[span] * gelu_slope(acc[span])).T.astype(bf16)

        @pl.when(core == 1)
        def _():
            turned[:, span] = gelu_value(other[span]).T.astype(bf16)

    def terms(step, carry):
        x, y_hi, z_hi = step // 4, lax.rem(step // 2, 2), lax.rem(step, 2)
        columns = pl.ds(pl.multiple_of(step * 768, 768), 768)
        part = jnp.dot(turned[...], act[:, columns], preferred_element_type=f32).astype(bf16)
        for z_lo in range(2):
            for p in range(3):
                for low in range(2):
                    start = (z_lo * 3 + p) * 128
                    grads[(p,) + block(p, x, y_hi * 2 + low, z_hi * 2 + z_lo)] = part[
                        low * 128 : low * 128 + 128, start : start + 128
                    ]
        return carry

    lax.fori_loop(0, 16, terms, 0)

    for step in STEPS:
        for p in range(3):
            one, two, three = places(p)
            for way in WAYS:
                send(
                    ("s1", p, way, step),
                    grads.at[p, ring(three, 2), ring(two, step), :, half(way, 128)],
                    first_rows.at[p, SIDE[way], SLOT[step]],
                    neighbours[ORDER[p][2], way],
                )

    def add_first(p, way, step):
        one, two, three = places(p)
        arrived(("s1", p, way, step))
        ref = grads.at[p, ring(three, way), ring(two, step), :, half(way, 128)]
        ref[...] = (ref[...].astype(f32) + first_rows[p, SIDE[way], SLOT[step]].astype(f32)).astype(bf16)

    for step in (2, 1, -1):
        for p in range(3):
            one, two, three = places(p)
            for way in WAYS:
                add_first(p, way, step)
                send(
                    ("s2", p, way, step),
                    grads.at[p, ring(three, way), ring(two, step)],
                    full_rows.at[p, SIDE[way], SLOT[step]],
                    neighbours[ORDER[p][2], way],
                )

    def send_own_row(p, way, step):
        one, two, three = places(p)
        send(
            ("s2u", p, way, step),
            grads.at[p, ring(three, way), two, ring(one, step)],
            full_units.at[p, SIDE[way], SLOT[step]],
            neighbours[ORDER[p][2], way],
        )

    for p in range(3):
        for way in WAYS:
            add_first(p, way, 0)
            send_own_row(p, way, 2)

    def sum_row(p, step):
        one, two, three = places(p)
        for way in WAYS:
            arrived(("s2", p, way, step))
        return (
            grads[p, three, ring(two, step)].astype(f32)
            + full_rows[p, 0, SLOT[step]].astype(f32)
            + full_rows[p, 1, SLOT[step]].astype(f32)
        )

    for p in range(3):
        one, two, three = places(p)
        grads[p, three, ring(two, 2)] = sum_row(p, 2).astype(bf16)
        for way in WAYS:
            send(
                ("s3", p, way),
                grads.at[p, three, ring(two, 2), :, half(way, 128)],
                first_second.at[p, SIDE[way]],
                neighbours[ORDER[p][1], way],
            )
    for step in WAYS:
        for p in range(3):
            for way in WAYS:
                send_own_row(p, way, step)

    for p in range(3):
        one, two, three = places(p)
        for way in WAYS:
            row = sum_row(p, way)
            arrived(("s3", p, way))
            low, high = row[:, :64], row[:, 64:]
            extra = first_second[p, SIDE[way]].astype(f32)
            low, high = (low + extra, high) if way == 1 else (low, high + extra)
            grads[p, three, ring(two, way), :, :64] = low.astype(bf16)
            grads[p, three, ring(two, way), :, 64:] = high.astype(bf16)
        for step in (2, 1, -1):
            for way in WAYS:
                send(
                    ("s4", p, way, step),
                    grads.at[p, three, ring(two, way), ring(one, step)],
                    second_units.at[p, SIDE[way], SLOT[step]],
                    neighbours[ORDER[p][1], way],
                )
    for p in range(3):
        one, two, three = places(p)
        for way in WAYS:
            send_own_row(p, way, 0)

    def sum_unit(p, step):
        one, two, three = places(p)
        total = grads[p, three, two, ring(one, step)].astype(f32)
        for way in WAYS:
            arrived(("s2u", p, way, step))
            total += full_units[p, SIDE[way], SLOT[step]].astype(f32)
        for way in WAYS:
            arrived(("s4", p, way, step))
            total += second_units[p, SIDE[way], SLOT[step]].astype(f32)
        return total

    for p in range(3):
        one, two, three = places(p)
        grads[p, three, two, ring(one, 2)] = sum_unit(p, 2).astype(bf16)
        for way in WAYS:
            send(
                ("s5", p, way),
                grads.at[p, three, two, ring(one, 2), half(way, 128)],
                first_last.at[p, SIDE[way]],
                neighbours[ORDER[p][0], way],
            )
    for p in range(3):
        one, two, three = places(p)
        for way in WAYS:
            send(
                ("s4", p, way, 0),
                grads.at[p, three, ring(two, way), one],
                second_units.at[p, SIDE[way], SLOT[0]],
                neighbours[ORDER[p][1], way],
            )
    for p in range(3):
        one, two, three = places(p)
        for way in WAYS:
            total = sum_unit(p, way)
            arrived(("s5", p, way))
            low, high = total[:64], total[64:]
            extra = first_last[p, SIDE[way]].astype(f32)
            low, high = (low + extra, high) if way == 1 else (low, high + extra)
            grads[p, three, two, ring(one, way), :64] = low.astype(bf16)
            grads[p, three, two, ring(one, way), 64:] = high.astype(bf16)
            send(
                ("s6", p, way),
                grads.at[p, three, two, ring(one, way)],
                last_unit.at[p, SIDE[way]],
                neighbours[ORDER[p][0], way],
            )
    for p in range(3):
        total = sum_unit(p, 0)
        for way in WAYS:
            arrived(("s6", p, way))
            total += last_unit[p, SIDE[way]].astype(f32)
        final[p * 128 : p * 128 + 128] = total.T

    index = y_lo * 2 + core
    for which in (3, 2, 1):
        to = lax.rem(y_lo + which // 2, 2) * 2 + lax.rem(core + which % 2, 2)
        send(
            ("end", which),
            final.at[pl.ds(pl.multiple_of(to * 96, 96), 96)],
            finals.at[index],
            partner(which),
        )
    finals[index] = final[pl.ds(pl.multiple_of(index * 96, 96), 96)]
    for which in (1, 2, 3):
        arrived(("end", which))
    for source in range(4):
        start = (source % 2) * 256 + (source // 2) * 128
        gradient_out[0, :, start : start + 128] = finals[source]

    for copy in messages.values():
        copy.wait_send()


def per_device(params, moment, second, grad_prev, tokens, cotangent):
    vmem = pl.BlockSpec(memory_space=pltpu.VMEM)
    shard = (1, 96, 512)
    n_messages = 300
    return pl.pallas_call(
        kernel,
        out_shape=(
            jax.ShapeDtypeStruct(shard, bf16),
            jax.ShapeDtypeStruct(shard, bf16),
            jax.ShapeDtypeStruct(shard, bf16),
            jax.ShapeDtypeStruct(shard, f32),
        ),
        in_specs=[vmem] * 4 + [pl.BlockSpec(memory_space=pl.ANY)] * 2,
        out_specs=(vmem,) * 4,
        scratch_shapes=[
            pltpu.VMEM((768, 12288), bf16),
            pltpu.VMEM((3, 4, 4, 4, 64, 256), bf16),
            pltpu.VMEM((3, 4, 4, 4, 128, 128), bf16),
            pltpu.VMEM((768, 256), f32),
            pltpu.VMEM((768, 256), f32),
            pltpu.VMEM((256, 768), bf16),
            pltpu.VMEM((3, 96, 256), bf16),
            pltpu.VMEM((3, 2, 4, 4, 64, 128), bf16),
            pltpu.VMEM((3, 2, 3, 4, 128, 128), bf16),
            pltpu.VMEM((3, 2, 4, 128, 128), bf16),
            pltpu.VMEM((3, 2, 4, 64, 128), bf16),
            pltpu.VMEM((3, 2, 4, 128, 128), bf16),
            pltpu.VMEM((3, 2, 64, 128), bf16),
            pltpu.VMEM((3, 2, 128, 128), bf16),
            pltpu.VMEM((384, 128), f32),
            pltpu.VMEM((4, 96, 128), f32),
            pltpu.SemaphoreType.DMA((n_messages,)),
            pltpu.SemaphoreType.DMA((n_messages,)),
            pltpu.SemaphoreType.DMA((3,)),
        ],
        compiler_params=pltpu.CompilerParams(
            collective_id=0, has_side_effects=True, vmem_limit_bytes=56 * 2**20
        ),
    )(params, moment, second, grad_prev, tokens, cotangent)


def solution(mesh):
    blocks = P("inner", "outer", None)
    rows = P(("outer", "inner"), None)
    return jax.shard_map(
        per_device,
        mesh=mesh,
        in_specs=(blocks,) * 4 + (rows,) * 2,
        out_specs=(blocks,) * 4,
        check_vma=False,
    )
```

```python
import functools

import jax
import jax.numpy as jnp
from jax import lax
from jax.experimental import pallas as pl
from jax.experimental.pallas import tpu as pltpu
from jax.sharding import PartitionSpec as P

beta_one = 0.9
beta_two = 0.95
bias_one = 0.9999734386011124
bias_two = 0.994079470779666
epsilon_adam = 1e-08
learn_rate = 6e-05
decay_rate = 0.1
root_scale = 0.7978845608028654
cubic_term = 0.044715

MESH = pl.DeviceIdType.MESH
f32 = jnp.float32
bf16 = jnp.bfloat16

ORDER = ((0, 1, 2), (1, 2, 0), (2, 0, 1))
STEPS = (2, 1, -1, 0)
SLOT = {2: 0, 1: 1, -1: 2, 0: 3}
WAYS = (1, -1)
SIDE = {1: 0, -1: 1}


def gelu_value(values):
    tangent = jnp.tanh(root_scale * (values + cubic_term * values * values * values))
    return 0.5 * values * (1.0 + tangent)


def gelu_slope(values):
    tangent = jnp.tanh(root_scale * (values + cubic_term * values * values * values))
    return 0.5 * (1.0 + tangent) + 0.5 * values * (1.0 - tangent * tangent) * root_scale * (
        1.0 + 3.0 * cubic_term * values * values
    )


def adam_update(params, moment, second, grad_prev):
    moment_new = beta_one * moment.astype(f32) + (1.0 - beta_one) * grad_prev
    second_new = beta_two * second.astype(f32) + (1.0 - beta_two) * grad_prev * grad_prev
    update = moment_new / bias_one / (
        jnp.sqrt(second_new / bias_two) + epsilon_adam
    ) + decay_rate * params.astype(f32)
    fresh = params.astype(f32) - learn_rate * update
    return (fresh.astype(bf16), moment_new.astype(bf16), second_new.astype(bf16))


def ring(place, step):
    return lax.rem(place + (step + 4), 4)


def device(x, y, z, core):
    return {"outer": z * 4 + lax.rem(y, 2) * 2 + core, "inner": x * 2 + y // 2}


GATHER = (
    *(("own", p, level) for level in range(3) for p in range(3)),
    *(step for p in range(3) for step in (("first", p), ("unit", p, 1, 1), ("unit", p, 1, -1))),
    *(("second", p, 0) for p in range(3)),
    *(("unit", p, 2, step) for p in range(3) for step in (1, -1)),
    *(("unit", p, 1, 2) for p in range(3)),
    *(("unit", p, 2, 2) for p in range(3)),
    *(("second", p, step) for p in range(3) for step in (1, -1)),
    *(("second", p, 2) for p in range(3)),
    *(("row", p, 1) for p in range(3)),
    *(("third", p, 0) for p in range(3)),
    *(("row", p, step) for p in range(3) for step in (2,)),
    *(("row", p, -1) for p in range(3)),
    *(("third", p, 1) for p in range(3)),
    *(("third", p, -1) for p in range(3)),
    ("mul", 0), ("mul", 1), ("mul", 2),
    *(("third", p, 2) for p in range(3)),
    ("mul", 3), ("mul", 4), ("mul", 5), ("mul", 6), ("mul", 7),
)
SCATTER = (
    ("terms", 0), ("first", 1, 2),
    ("terms", 1), ("first", 1, 1), ("first", 2, 2), ("first", 1, -1), ("first", 1, 0),
    ("terms", 2), ("first", 0, 2), ("first", 0, 1), ("first", 0, -1), ("first", 0, 0),
    ("terms", 3), ("first", 2, 1), ("terms", 4), ("first", 2, -1), ("terms", 5), ("first", 2, 0),
    *(("row", p, 2) for p in range(3)),
    *(("row", p, 1) for p in range(3)),
    *(step for p in range(3) for step in (("row", p, -1), ("second", p))),
    *(("own", p, 2) for p in range(3)),
    *(step for p in range(3) for step in (("add", p), ("unit", p, 2), ("unit", p, 1), ("unit", p, -1))),
    *(("own", p, step) for step in (1, -1) for p in range(3)),
    *(("third", p) for p in range(3)),
    *(("own", p, 0) for p in range(3)),
    *(("unit", p, 0) for p in range(3)),
    *(("last", p) for p in range(3)),
    *(("end", p) for p in range(3)),
)


def kernel(
    params, moment, second, grad_prev, tokens, cotangent,
    gradient_out,
    act, held, grads, acc, other, turned, stage,
    old_params, old_moment, old_second, old_grad,
    first_rows, full_rows, full_units, first_second, second_units, first_last, last_unit,
    final, finals, send_sems, recv_sems, local_sems,
):
    outer = lax.axis_index("outer")
    inner = lax.axis_index("inner")
    core = lax.rem(outer, 2)
    y_lo = lax.rem(outer // 2, 2)
    y_hi = lax.rem(inner, 2)
    own = (inner // 2, y_hi * 2 + y_lo, outer // 4)

    def neighbour(axis, way):
        place = list(own)
        place[axis] = ring(place[axis], way)
        return device(*place, core)

    def partner(which):
        return device(
            own[0], own[1] - y_lo + lax.rem(y_lo + which // 2, 2), own[2], lax.rem(core + which % 2, 2)
        )

    neighbours = {(axis, way): neighbour(axis, way) for axis in range(3) for way in WAYS}
    sibling = partner(1)

    barrier = pltpu.get_barrier_semaphore()
    greeted = list(neighbours.values()) + [sibling, partner(3)]
    for one in greeted:
        pl.semaphore_signal(barrier, inc=1, device_id=one, device_id_type=MESH)

    old = [
        pltpu.make_async_copy(source.at[0], target, local_sems.at[3 + index])
        for index, (source, target) in enumerate(
            ((params, old_params), (moment, old_moment), (second, old_second), (grad_prev, old_grad))
        )
    ]
    for copy in old:
        copy.start()

    mine = pl.ds(pl.multiple_of(core * 384, 384), 384)

    def load_own(source):
        return pltpu.make_async_copy(source, act.at[mine], local_sems.at[0])

    @pl.when(core == 0)
    def _():
        load_own(tokens).start()

    @pl.when(core == 1)
    def _():
        load_own(cotangent).start()

    groups = {}
    seen = set()
    leaving = {
        "rows": (0, stage.at[0]),
        "g1": (1, held.at[:, 0, 0, 0:3]), "g1f": (1,), "g2": (2, held.at[:, 0, 0:3]), "g2f": (2,),
        "g3": (3, held.at[:, 0:3]), "g3r": (3,), "g3f": (3,),
        "products": (4, acc),
        "s1": (5, grads.at[:, 0:3]), "s2": (5,), "s2u": (5,), "s3": (6, grads.at[:, 0, 0:3]), "s4": (6,),
        "s5": (7, grads.at[:, 0, 0, 0:3]), "s6": (7,),
        "end": (8, finals.at[0:3]),
    }

    def coming(key):
        name, p = key[0], key[1]
        if name in ("rows", "end"):
            return (name,), stage.at[2] if name == "rows" else finals.at[0:3]
        if name == "products":
            return key, other.at[0:384]
        if name == "g3f":
            return (name, key[3]), held.at[:, 0, 0]
        ref = held if name[0] == "g" else grads
        if name in ("g1", "s6"):
            return (name, p), ref.at[p, 0, 0, 0:2]
        if name in ("g1f", "s5"):
            return (name, p), ref.at[p, 0, 0, 0]
        if name in ("g2f", "s3"):
            return (name, p), ref.at[p, 0, 0]
        if name == "g3":
            return (name, p), ref.at[p, 0, 0:2]
        if name in ("g2", "s2u", "s4"):
            return (name, p, key[3]), ref.at[p, 0, 0, 0:2]
        if name == "s1":
            return (name, p, key[3]), ref.at[p, 0, 0]
        return (name, p, key[3]), ref.at[p, 0, 0:2]

    def send(key, source, target, to):
        group = coming(key)[0]
        index = groups.setdefault(group, len(groups))
        pltpu.make_async_remote_copy(
            src_ref=source,
            dst_ref=target,
            send_sem=send_sems.at[leaving[key[0]][0]],
            recv_sem=recv_sems.at[index],
            device_id=to,
            device_id_type=MESH,
        ).start()

    def arrived(*keys):
        for key in keys:
            group, view = coming(key)
            if group not in seen:
                seen.add(group)
                pltpu.make_async_copy(view, view, recv_sems.at[groups[group]]).wait()

    for copy in old:
        copy.wait()

    def fresh(columns):
        return adam_update(
            old_params[:, columns], old_moment[:, columns], old_second[:, columns], old_grad[:, columns]
        )[0]

    stage[0] = fresh(slice(0, 256))
    stage[1] = fresh(slice(256, 512))

    pl.semaphore_wait(barrier, len(greeted))

    send(("rows", 0), stage.at[1 - core], stage.at[2], sibling)

    def load_sibling(source):
        return pltpu.make_async_remote_copy(
            src_ref=source,
            dst_ref=act.at[mine],
            send_sem=local_sems.at[1],
            recv_sem=local_sems.at[2],
            device_id=sibling,
            device_id_type=MESH,
        )

    @pl.when(core == 0)
    def _():
        load_sibling(cotangent).start()

    @pl.when(core == 1)
    def _():
        load_sibling(tokens).start()

    def places(p):
        return tuple(own[axis] for axis in ORDER[p])

    arrived(("rows", 0))
    for first_core in range(2):
        @pl.when(core == first_core)
        def _():
            low, high = (stage[first_core], stage[2]) if first_core == 0 else (stage[2], stage[first_core])
            pieces = (low[:64], jnp.concatenate([low[64:], high[:32]], axis=0), high[32:])
            for p in range(3):
                one, two, three = places(p)
                held[p, three, two, one] = pieces[p]

    def half(way, rows):
        return pl.ds(SIDE[way] * (rows // 2), rows // 2)

    def unit(p, three, two, one):
        return held.at[p, three, two, one]

    def give(key, p, level, ref):
        for way in WAYS:
            send((key[0], p, way) + key[1:], ref, ref, neighbours[ORDER[p][level], way])

    def pass_on(key, p, level, way, ref):
        send(key, ref, ref, neighbours[ORDER[p][level], way])

    def give_own(p, level):
        one, two, three = places(p)
        give((f"g{level + 1}",) + ((0,) if level else ()), p, level, unit(p, three, two, one))

    def pass_first(p):
        one, two, three = places(p)
        for way in WAYS:
            arrived(("g1", p, way))
            pass_on(("g1f", p, way), p, 0, way, held.at[p, three, two, ring(one, -way), half(way, 64)])

    def give_unit(p, level, step):
        one, two, three = places(p)
        arrived(("g1f" if step == 2 else "g1", p, 1))
        give((f"g{level + 1}", step), p, level, unit(p, three, two, ring(one, step)))

    def pass_second(p, step):
        one, two, three = places(p)
        for way in WAYS:
            arrived(("g2", p, way, step))
            pass_on(
                ("g2f", p, way, step), p, 1, way,
                held.at[p, three, ring(two, -way), ring(one, step), half(way, 64)],
            )

    def give_row(p, step):
        one, two, three = places(p)
        if step == 2:
            arrived(*[("g2f", p, way, k) for way in WAYS for k in STEPS])
        else:
            arrived(*[("g2", p, -step, k) for k in STEPS])
        give(("g3r", step), p, 2, held.at[p, three, ring(two, step)])

    def third(p, way, step):
        return [("g3", p, way, k) for k in STEPS] if step == 0 else [("g3r", p, way, step)]

    def pass_third(p, step):
        one, two, three = places(p)
        for way in WAYS:
            arrived(*third(p, way, step))
            pass_on(
                ("g3f", p, way, step), p, 2, way,
                held.at[p, ring(three, -way), ring(two, step), :, half(way, 64)],
            )

    def block(p, x, y, z):
        place = (x, y, z)
        return tuple(place[axis] for axis in reversed(ORDER[p]))

    def columns(x, part, z):
        return pl.ds(pl.multiple_of(x * 3072 + part * 1536 + z * 384, 128), 384)

    def chunk_product(chunks, rows=slice(None)):
        left, right = [], []
        for step_x, flip, step_z in chunks:
            x, part, z = ring(own[0], step_x), lax.rem(y_hi + flip, 2), ring(own[2], step_z)
            left.append(act[rows, columns(x, part, z)])
            right += [held[(p,) + block(p, x, part * 2 + low, z)] for low in range(2) for p in range(3)]
        return jnp.dot(
            jnp.concatenate(left, axis=1), jnp.concatenate(right, axis=0), preferred_element_type=f32
        )

    near = (0, 1, -1)

    def multiply(which):
        if "loaded" not in seen:
            seen.add("loaded")
            load_own(tokens).wait()
            load_sibling(tokens).wait()
        for p in range(3):
            arrived(("g1", p, 1), ("g1f", p, 1), *[("g2", p, 1, k) for k in STEPS])
            if which >= 3:
                arrived(("g2f", p, 1, 0))
            for way in WAYS:
                for step in near:
                    arrived(*third(p, way, step))
                if which >= 3:
                    arrived(*third(p, way, 2))
                    for step in near[: which - 2]:
                        arrived(("g3f", p, way, step))
        if which < 3:
            todo = [(near[which], 0, z) for z in near]
        elif which < 6:
            todo = [(near[which - 3], 1, z) for z in near]
        elif which == 6:
            todo = [(2, 0, z) for z in near]
        else:
            todo = [(x, 0, 2) for x in near]
        part = chunk_product(todo)
        if which:
            acc[...] += part
        else:
            acc[...] = part

    actions = {
        "own": give_own, "first": pass_first, "unit": give_unit, "second": pass_second,
        "row": give_row, "third": pass_third, "mul": multiply,
    }
    for name, *rest in GATHER:
        actions[name](*rest)
    for p in range(3):
        for way in WAYS:
            arrived(("g3f", p, way, 2))
    last = [(2, 0, 2)] + [(2, 1, z) for z in (0, 1, -1, 2)] + [(x, 1, 2) for x in near]
    for index in range(2):
        rows = slice(index * 384, index * 384 + 384)
        acc[rows] += chunk_product(last, rows)
        send(("products", index), acc.at[rows], other.at[rows], sibling)
    for index in range(2):
        arrived(("products", index))
        for start in range(index * 384, index * 384 + 384, 128):
            span = slice(start, start + 128)

            @pl.when(core == 0)
            def _():
                turned[:, span] = (other[span] * gelu_slope(acc[span])).T.astype(bf16)

            @pl.when(core == 1)
            def _():
                turned[:, span] = gelu_value(other[span]).T.astype(bf16)

    def term(x, z):
        right = jnp.concatenate([act[:, columns(x, part, z)] for part in range(2)], axis=1)
        result = jnp.dot(turned[...], right, preferred_element_type=f32).astype(bf16)
        for part in range(2):
            for p in range(3):
                for low in range(2):
                    start = (part * 3 + p) * 128
                    grads[(p,) + block(p, x, part * 2 + low, z)] = result[
                        low * 128 : low * 128 + 128, start : start + 128
                    ]

    def terms(which):
        x, z = own[0], own[2]
        if which == 0:
            term(ring(x, 2), ring(z, 2))
        else:
            def body(step, carry):
                off = step - 1
                if which == 1:
                    term(ring(x, 2), ring(z, off))
                elif which == 2:
                    term(ring(x, off), ring(z, 2))
                else:
                    term(ring(x, (1, -1, 0)[which - 3]), ring(z, off))
                return carry

            lax.fori_loop(0, 3, body, 0)

    def send_first(p, step):
        one, two, three = places(p)
        for way in WAYS:
            send(
                ("s1", p, way, step),
                grads.at[p, ring(three, 2), ring(two, step), :, half(way, 128)],
                first_rows.at[p, SIDE[way], SLOT[step]],
                neighbours[ORDER[p][2], way],
            )

    def add_first(p, way, step):
        one, two, three = places(p)
        arrived(("s1", p, way, step))
        ref = grads.at[p, ring(three, way), ring(two, step), :, half(way, 128)]
        ref[...] = (ref[...].astype(f32) + first_rows[p, SIDE[way], SLOT[step]].astype(f32)).astype(bf16)

    def send_row(p, step):
        one, two, three = places(p)
        for way in WAYS:
            add_first(p, way, step)
            send(
                ("s2", p, way, step),
                grads.at[p, ring(three, way), ring(two, step)],
                full_rows.at[p, SIDE[way], SLOT[step]],
                neighbours[ORDER[p][2], way],
            )

    def send_own_row(p, step):
        one, two, three = places(p)
        for way in WAYS:
            if ("added", p, way) not in seen:
                seen.add(("added", p, way))
                add_first(p, way, 0)
            send(
                ("s2u", p, way, step),
                grads.at[p, ring(three, way), two, ring(one, step)],
                full_units.at[p, SIDE[way], SLOT[step]],
                neighbours[ORDER[p][2], way],
            )

    def sum_row(p, step):
        one, two, three = places(p)
        arrived(*[("s2", p, way, step) for way in WAYS])
        return (
            grads[p, three, ring(two, step)].astype(f32)
            + full_rows[p, 0, SLOT[step]].astype(f32)
            + full_rows[p, 1, SLOT[step]].astype(f32)
        )

    def send_second(p):
        one, two, three = places(p)
        grads[p, three, ring(two, 2)] = sum_row(p, 2).astype(bf16)
        for way in WAYS:
            send(
                ("s3", p, way),
                grads.at[p, three, ring(two, 2), :, half(way, 128)],
                first_second.at[p, SIDE[way]],
                neighbours[ORDER[p][1], way],
            )

    def add_second(p):
        one, two, three = places(p)
        for way in WAYS:
            row = sum_row(p, way)
            arrived(("s3", p, way))
            low, high = row[:, :64], row[:, 64:]
            extra = first_second[p, SIDE[way]].astype(f32)
            low, high = (low + extra, high) if way == 1 else (low, high + extra)
            grads[p, three, ring(two, way), :, :64] = low.astype(bf16)
            grads[p, three, ring(two, way), :, 64:] = high.astype(bf16)

    def send_unit(p, step):
        one, two, three = places(p)
        for way in WAYS:
            send(
                ("s4", p, way, step),
                grads.at[p, three, ring(two, way), ring(one, step)],
                second_units.at[p, SIDE[way], SLOT[step]],
                neighbours[ORDER[p][1], way],
            )

    def sum_unit(p, step):
        one, two, three = places(p)
        total = grads[p, three, two, ring(one, step)].astype(f32)
        for way in WAYS:
            arrived(("s2u", p, way, step))
            total += full_units[p, SIDE[way], SLOT[step]].astype(f32)
        for way in WAYS:
            arrived(("s4", p, way, step))
            total += second_units[p, SIDE[way], SLOT[step]].astype(f32)
        return total

    def send_third(p):
        one, two, three = places(p)
        grads[p, three, two, ring(one, 2)] = sum_unit(p, 2).astype(bf16)
        for way in WAYS:
            send(
                ("s5", p, way),
                grads.at[p, three, two, ring(one, 2), half(way, 128)],
                first_last.at[p, SIDE[way]],
                neighbours[ORDER[p][0], way],
            )

    def send_last(p):
        one, two, three = places(p)
        for way in WAYS:
            total = sum_unit(p, way)
            arrived(("s5", p, way))
            low, high = total[:64], total[64:]
            extra = first_last[p, SIDE[way]].astype(f32)
            low, high = (low + extra, high) if way == 1 else (low, high + extra)
            grads[p, three, two, ring(one, way), :64] = low.astype(bf16)
            grads[p, three, two, ring(one, way), 64:] = high.astype(bf16)
            send(
                ("s6", p, way),
                grads.at[p, three, two, ring(one, way)],
                last_unit.at[p, SIDE[way]],
                neighbours[ORDER[p][0], way],
            )

    def finish(p):
        total = sum_unit(p, 0)
        for way in WAYS:
            arrived(("s6", p, way))
            total += last_unit[p, SIDE[way]].astype(f32)
        final[p * 128 : p * 128 + 128] = total.T

    actions = {
        "terms": terms, "first": send_first, "row": send_row, "own": send_own_row, "second": send_second,
        "add": add_second, "unit": send_unit, "third": send_third, "last": send_last, "end": finish,
    }
    for name, *rest in SCATTER:
        actions[name](*rest)

    index = y_lo * 2 + core
    for which in (3, 2, 1):
        to = lax.rem(y_lo + which // 2, 2) * 2 + lax.rem(core + which % 2, 2)
        send(
            ("end", which),
            final.at[pl.ds(pl.multiple_of(to * 96, 96), 96)],
            finals.at[index],
            partner(which),
        )
    finals[index] = final[pl.ds(pl.multiple_of(index * 96, 96), 96)]
    for which in (1, 2, 3):
        arrived(("end", which))
    for source in range(4):
        start = (source % 2) * 256 + (source // 2) * 128
        gradient_out[0, :, start : start + 128] = finals[source]

    for index, *view in leaving.values():
        if view:
            pltpu.make_async_copy(view[0], view[0], send_sems.at[index]).wait()


def per_device(params, moment, second, grad_prev, tokens, cotangent):
    shard = (1, 96, 512)
    gradient = pl.pallas_call(
        kernel,
        out_shape=jax.ShapeDtypeStruct(shard, f32),
        in_specs=[pl.BlockSpec(memory_space=pl.ANY)] * 6,
        out_specs=pl.BlockSpec(memory_space=pltpu.VMEM),
        scratch_shapes=[
            pltpu.VMEM((768, 12288), bf16),
            pltpu.VMEM((3, 4, 4, 4, 64, 256), bf16),
            pltpu.VMEM((3, 4, 4, 4, 128, 128), bf16),
            pltpu.VMEM((768, 256), f32),
            pltpu.VMEM((768, 256), f32),
            pltpu.VMEM((256, 768), bf16),
            pltpu.VMEM((3, 96, 256), bf16),
            pltpu.VMEM((96, 512), bf16),
            pltpu.VMEM((96, 512), bf16),
            pltpu.VMEM((96, 512), bf16),
            pltpu.VMEM((96, 512), f32),
            pltpu.VMEM((3, 2, 4, 4, 64, 128), bf16),
            pltpu.VMEM((3, 2, 3, 4, 128, 128), bf16),
            pltpu.VMEM((3, 2, 4, 128, 128), bf16),
            pltpu.VMEM((3, 2, 4, 64, 128), bf16),
            pltpu.VMEM((3, 2, 4, 128, 128), bf16),
            pltpu.VMEM((3, 2, 64, 128), bf16),
            pltpu.VMEM((3, 2, 128, 128), bf16),
            pltpu.VMEM((384, 128), f32),
            pltpu.VMEM((4, 96, 128), f32),
            pltpu.SemaphoreType.DMA((9,)),
            pltpu.SemaphoreType.DMA((95,)),
            pltpu.SemaphoreType.DMA((7,)),
        ],
        compiler_params=pltpu.CompilerParams(
            collective_id=0, has_side_effects=True, vmem_limit_bytes=56 * 2**20
        ),
    )(params, moment, second, grad_prev, tokens, cotangent)
    return adam_update(params, moment, second, grad_prev) + (gradient,)


def solution(mesh):
    blocks = P("inner", "outer", None)
    rows = P(("outer", "inner"), None)
    return jax.shard_map(
        per_device,
        mesh=mesh,
        in_specs=(blocks,) * 4 + (rows,) * 2,
        out_specs=(blocks,) * 4,
        check_vma=False,
    )
```

```python
import functools

import jax
import jax.numpy as jnp
from jax import lax
from jax.experimental import pallas as pl
from jax.experimental.pallas import tpu as pltpu
from jax.sharding import PartitionSpec as P

beta_one = 0.9
beta_two = 0.95
bias_one = 0.9999734386011124
bias_two = 0.994079470779666
epsilon_adam = 1e-08
learn_rate = 6e-05
decay_rate = 0.1
root_scale = 0.7978845608028654
cubic_term = 0.044715

MESH = pl.DeviceIdType.MESH
f32 = jnp.float32
bf16 = jnp.bfloat16

ORDER = ((0, 1, 2), (1, 2, 0), (2, 0, 1))
STEPS = (2, 1, -1, 0)
SLOT = {2: 0, 1: 1, -1: 2, 0: 3}
WAYS = (1, -1)
SIDE = {1: 0, -1: 1}


def gelu_value(values):
    tangent = jnp.tanh(root_scale * (values + cubic_term * values * values * values))
    return 0.5 * values * (1.0 + tangent)


def gelu_slope(values):
    tangent = jnp.tanh(root_scale * (values + cubic_term * values * values * values))
    return 0.5 * (1.0 + tangent) + 0.5 * values * (1.0 - tangent * tangent) * root_scale * (
        1.0 + 3.0 * cubic_term * values * values
    )


def adam_update(params, moment, second, grad_prev):
    moment_new = beta_one * moment.astype(f32) + (1.0 - beta_one) * grad_prev
    second_new = beta_two * second.astype(f32) + (1.0 - beta_two) * grad_prev * grad_prev
    update = moment_new / bias_one / (
        jnp.sqrt(second_new / bias_two) + epsilon_adam
    ) + decay_rate * params.astype(f32)
    fresh = params.astype(f32) - learn_rate * update
    return (fresh.astype(bf16), moment_new.astype(bf16), second_new.astype(bf16))


def ring(place, step):
    return lax.rem(place + (step + 4), 4)


def device(x, y, z, core):
    return {"outer": z * 4 + lax.rem(y, 2) * 2 + core, "inner": x * 2 + y // 2}


GATHER = (
    ("own", 1, 0), ("own", 0, 0), ("own", 2, 0), ("own", 2, 2), ("own", 0, 2), ("own", 1, 1), ("own", 2, 1),
    ("own", 1, 2), ("own", 0, 1), ("first", 1), ("first", 0), ("first", 2), ("unit", 0, 1, -1), ("unit", 1, 1, -1),
    ("unit", 0, 1, 1), ("unit", 2, 1, 1), ("unit", 2, 2, -1), ("unit", 2, 1, -1), ("unit", 0, 2, 1),
    ("unit", 1, 2, 1), ("second", 2, 0), ("unit", 1, 1, 1), ("unit", 1, 1, 2), ("unit", 0, 1, 2), ("unit", 2, 2, 1),
    ("unit", 2, 1, 2), ("unit", 0, 2, 2), ("unit", 2, 2, 2), ("second", 0, -1), ("unit", 1, 2, -1), ("second", 0, 0),
    ("second", 1, -1), ("unit", 0, 2, -1), ("second", 0, 1), ("second", 1, 0), ("second", 2, 1), ("second", 2, -1),
    ("second", 1, 1), ("unit", 1, 2, 2), ("second", 1, 2), ("row", 1, -1), ("second", 0, 2), ("row", 0, -1),
    ("row", 2, -1), ("row", 2, 1), ("row", 0, 1), ("second", 2, 2), ("row", 1, 1), ("third", 1, 0), ("row", 1, 2),
    ("row", 2, 2), ("row", 0, 2), ("third", 2, 0), ("third", 0, 0), ("mul", 0), ("third", 1, 1), ("third", 2, 1),
    ("third", 0, 1), ("mul", 2), ("third", 0, -1), ("third", 1, -1), ("third", 2, -1), ("mul", 1), ("mul", 3),
    ("third", 0, 2), ("third", 2, 2), ("third", 1, 2), ("mul", 4), ("mul", 5), ("mul", 6), ("mul", 7),
)
SCATTER = (
    ("terms", 0), ("first", 1, 2), ("terms", 1), ("first", 1, 1), ("first", 2, 2), ("first", 1, -1), ("first", 1, 0),
    ("terms", 2), ("first", 0, 2), ("first", 0, 1), ("first", 0, -1), ("first", 0, 0), ("terms", 3), ("first", 2, 1),
    ("terms", 4), ("first", 2, -1), ("terms", 5), ("first", 2, 0), ("row", 0, 2), ("row", 1, 2), ("row", 2, 2),
    ("row", 0, 1), ("row", 1, 1), ("row", 2, 1), ("row", 0, -1), ("second", 0), ("row", 1, -1), ("second", 1),
    ("row", 2, -1), ("second", 2), ("own", 0, 2), ("own", 1, 2), ("own", 2, 2), ("add", 0), ("unit", 0, 2),
    ("unit", 0, 1), ("unit", 0, -1), ("add", 1), ("unit", 1, 2), ("unit", 1, 1), ("unit", 1, -1), ("add", 2),
    ("unit", 2, 2), ("unit", 2, 1), ("unit", 2, -1), ("own", 0, 1), ("own", 1, 1), ("own", 2, 1), ("own", 0, -1),
    ("own", 1, -1), ("own", 2, -1), ("third", 0), ("third", 1), ("third", 2), ("own", 0, 0), ("own", 1, 0),
    ("own", 2, 0), ("unit", 0, 0), ("unit", 1, 0), ("unit", 2, 0), ("last", 0), ("last", 1), ("last", 2), ("end", 0),
    ("end", 1), ("end", 2),
)


def kernel(
    params, moment, second, grad_prev, tokens, cotangent,
    gradient_out,
    act, held, grads, acc, other, factor, stage,
    old_params, old_moment, old_second, old_grad,
    first_rows, full_rows, full_units, first_second, second_units, first_last, last_unit,
    final, finals, send_sems, recv_sems, local_sems,
):
    outer = lax.axis_index("outer")
    inner = lax.axis_index("inner")
    core = lax.rem(outer, 2)
    y_lo = lax.rem(outer // 2, 2)
    y_hi = lax.rem(inner, 2)
    own = (inner // 2, y_hi * 2 + y_lo, outer // 4)

    def neighbour(axis, way):
        place = list(own)
        place[axis] = ring(place[axis], way)
        return device(*place, core)

    neighbours = {(axis, way): neighbour(axis, way) for axis in range(3) for way in WAYS}
    sibling = device(*own, 1 - core)

    barrier = pltpu.get_barrier_semaphore()
    greeted = list(neighbours.values()) + [sibling]
    for one in greeted:
        pl.semaphore_signal(barrier, inc=1, device_id=one, device_id_type=MESH)

    old = [
        pltpu.make_async_copy(source.at[0], target, local_sems.at[3 + index])
        for index, (source, target) in enumerate(
            ((params, old_params), (moment, old_moment), (second, old_second), (grad_prev, old_grad))
        )
    ]
    for copy in old:
        copy.start()

    mine = pl.ds(pl.multiple_of(core * 384, 384), 384)

    def load_own(source):
        return pltpu.make_async_copy(source, act.at[mine], local_sems.at[0])

    @pl.when(core == 0)
    def _():
        load_own(tokens).start()

    @pl.when(core == 1)
    def _():
        load_own(cotangent).start()

    groups = {}
    seen = set()
    leaving = {
        "rows": (0, stage.at[0]),
        "g1": (1, held.at[:, 0, 0, 0:3]), "g1f": (1,), "g2": (2, held.at[:, 0, 0:3]), "g2f": (2,),
        "g3": (3, held.at[:, 0:3]), "g3r": (3,), "g3f": (3,),
        "products": (4, acc),
        "s1": (5, grads.at[:, 0:3]), "s2": (5,), "s2u": (5,), "s3": (6, grads.at[:, 0, 0:3]), "s4": (6,),
        "s5": (7, grads.at[:, 0, 0, 0:3]), "s6": (7,),
        "end": (8, finals),
    }

    def coming(key):
        name, p = key[0], key[1]
        if name in ("rows", "end"):
            return (name,), stage.at[2] if name == "rows" else finals
        if name == "products":
            return key, other.at[0:384]
        if name == "g3f":
            return (name, key[3]), held.at[:, 0, 0]
        ref = held if name[0] == "g" else grads
        if name in ("g1", "s6"):
            return (name, p), ref.at[p, 0, 0, 0:2]
        if name in ("g1f", "s5"):
            return (name, p), ref.at[p, 0, 0, 0]
        if name in ("g2f", "s3"):
            return (name, p), ref.at[p, 0, 0]
        if name == "g3":
            return (name, p), ref.at[p, 0, 0:2]
        if name in ("g2", "s2u", "s4"):
            return (name, p, key[3]), ref.at[p, 0, 0, 0:2]
        if name == "s1":
            return (name, p, key[3]), ref.at[p, 0, 0]
        return (name, p, key[3]), ref.at[p, 0, 0:2]

    def send(key, source, target, to):
        group = coming(key)[0]
        index = groups.setdefault(group, len(groups))
        pltpu.make_async_remote_copy(
            src_ref=source,
            dst_ref=target,
            send_sem=send_sems.at[leaving[key[0]][0]],
            recv_sem=recv_sems.at[index],
            device_id=to,
            device_id_type=MESH,
        ).start()

    def arrived(*keys):
        for key in keys:
            group, view = coming(key)
            if group not in seen:
                seen.add(group)
                pltpu.make_async_copy(view, view, recv_sems.at[groups[group]]).wait()

    for copy in old:
        copy.wait()

    def fresh(columns):
        return adam_update(
            old_params[:, columns], old_moment[:, columns], old_second[:, columns], old_grad[:, columns]
        )[0]

    stage[0] = fresh(slice(0, 256))
    stage[1] = fresh(slice(256, 512))

    pl.semaphore_wait(barrier, len(greeted))

    send(("rows", 0), stage.at[1 - core], stage.at[2], sibling)

    def load_sibling(source):
        return pltpu.make_async_remote_copy(
            src_ref=source,
            dst_ref=act.at[mine],
            send_sem=local_sems.at[1],
            recv_sem=local_sems.at[2],
            device_id=sibling,
            device_id_type=MESH,
        )

    @pl.when(core == 0)
    def _():
        load_sibling(cotangent).start()

    @pl.when(core == 1)
    def _():
        load_sibling(tokens).start()

    def places(p):
        return tuple(own[axis] for axis in ORDER[p])

    arrived(("rows", 0))
    for first_core in range(2):
        @pl.when(core == first_core)
        def _():
            low, high = (stage[first_core], stage[2]) if first_core == 0 else (stage[2], stage[first_core])
            pieces = (low[:64], jnp.concatenate([low[64:], high[:32]], axis=0), high[32:])
            for p in range(3):
                one, two, three = places(p)
                held[p, three, two, one] = pieces[p]

    def half(way, rows):
        return pl.ds(SIDE[way] * (rows // 2), rows // 2)

    def unit(p, three, two, one):
        return held.at[p, three, two, one]

    def give(key, p, level, ref):
        for way in WAYS:
            send((key[0], p, way) + key[1:], ref, ref, neighbours[ORDER[p][level], way])

    def pass_on(key, p, level, way, ref):
        send(key, ref, ref, neighbours[ORDER[p][level], way])

    def give_own(p, level):
        one, two, three = places(p)
        give((f"g{level + 1}",) + ((0,) if level else ()), p, level, unit(p, three, two, one))

    def pass_first(p):
        one, two, three = places(p)
        for way in WAYS:
            arrived(("g1", p, way))
            pass_on(("g1f", p, way), p, 0, way, held.at[p, three, two, ring(one, -way), half(way, 64)])

    def give_unit(p, level, step):
        one, two, three = places(p)
        arrived(("g1f" if step == 2 else "g1", p, 1))
        give((f"g{level + 1}", step), p, level, unit(p, three, two, ring(one, step)))

    def pass_second(p, step):
        one, two, three = places(p)
        for way in WAYS:
            arrived(("g2", p, way, step))
            pass_on(
                ("g2f", p, way, step), p, 1, way,
                held.at[p, three, ring(two, -way), ring(one, step), half(way, 64)],
            )

    def give_row(p, step):
        one, two, three = places(p)
        if step == 2:
            arrived(*[("g2f", p, way, k) for way in WAYS for k in STEPS])
        else:
            arrived(*[("g2", p, -step, k) for k in STEPS])
        give(("g3r", step), p, 2, held.at[p, three, ring(two, step)])

    def third(p, way, step):
        return [("g3", p, way, k) for k in STEPS] if step == 0 else [("g3r", p, way, step)]

    def pass_third(p, step):
        one, two, three = places(p)
        for way in WAYS:
            arrived(*third(p, way, step))
            pass_on(
                ("g3f", p, way, step), p, 2, way,
                held.at[p, ring(three, -way), ring(two, step), :, half(way, 64)],
            )

    def block(p, x, y, z):
        place = (x, y, z)
        return tuple(place[axis] for axis in reversed(ORDER[p]))

    def columns(x, part, z):
        return pl.ds(pl.multiple_of(x * 3072 + part * 1536 + z * 384, 128), 384)

    def chunk_product(chunks, rows=slice(None)):
        left, right = [], []
        for step_x, flip, step_z in chunks:
            x, part, z = ring(own[0], step_x), lax.rem(y_hi + flip, 2), ring(own[2], step_z)
            left.append(act[rows, columns(x, part, z)])
            right += [held[(p,) + block(p, x, part * 2 + low, z)] for low in range(2) for p in range(3)]
        return jnp.dot(
            jnp.concatenate(left, axis=1), jnp.concatenate(right, axis=0), preferred_element_type=f32
        )

    near = (0, 1, -1)

    def multiply(which):
        if "loaded" not in seen:
            seen.add("loaded")
            load_own(tokens).wait()
            load_sibling(tokens).wait()
        for p in range(3):
            arrived(("g1", p, 1), ("g1f", p, 1), *[("g2", p, 1, k) for k in STEPS])
            if which >= 3:
                arrived(("g2f", p, 1, 0))
            for way in WAYS:
                for step in near:
                    arrived(*third(p, way, step))
                if which >= 3:
                    arrived(*third(p, way, 2))
                    for step in near[: which - 2]:
                        arrived(("g3f", p, way, step))
        if which < 3:
            todo = [(near[which], 0, z) for z in near]
        elif which < 6:
            todo = [(near[which - 3], 1, z) for z in near]
        elif which == 6:
            todo = [(2, 0, z) for z in near]
        else:
            todo = [(x, 0, 2) for x in near]
        part = chunk_product(todo)
        if which:
            acc[...] += part
        else:
            acc[...] = part

    actions = {
        "own": give_own, "first": pass_first, "unit": give_unit, "second": pass_second,
        "row": give_row, "third": pass_third, "mul": multiply,
    }
    for name, *rest in GATHER:
        actions[name](*rest)
    for p in range(3):
        for way in WAYS:
            arrived(("g3f", p, way, 2))
    last = [(2, 0, 2)] + [(2, 1, z) for z in (0, 1, -1, 2)] + [(x, 1, 2) for x in near]
    for index in range(2):
        rows = slice(index * 384, index * 384 + 384)
        acc[rows] += chunk_product(last, rows)
        send(("products", index), acc.at[rows], other.at[rows], sibling)
    for index in range(2):
        arrived(("products", index))
        for start in range(index * 384, index * 384 + 384, 128):
            span = slice(start, start + 128)

            @pl.when(core == 0)
            def _():
                factor[span] = (other[span] * gelu_slope(acc[span])).astype(bf16)

            @pl.when(core == 1)
            def _():
                factor[span] = gelu_value(other[span]).astype(bf16)

    def term(x, z):
        for part in range(2):
            result = lax.dot_general(
                act[:, columns(x, part, z)], factor[...], (((0,), (0,)), ((), ())), preferred_element_type=f32
            ).astype(bf16)
            for low in range(2):
                for p in range(3):
                    start = (low * 3 + p) * 64
                    grads[(p,) + block(p, x, part * 2 + low, z)] = result[start : start + 64]

    def terms(which):
        x, z = own[0], own[2]
        if which == 0:
            term(ring(x, 2), ring(z, 2))
            return

        def body(index, carry):
            step = index - 1
            if which < 2:
                term(ring(x, 2), ring(z, step))
            elif which == 2:
                term(ring(x, step), ring(z, 2))
            else:
                term(ring(x, (1, -1, 0)[which - 3]), ring(z, step))
            return carry

        lax.fori_loop(0, 3, body, 0)

    def send_first(p, step):
        one, two, three = places(p)
        for way in WAYS:
            send(
                ("s1", p, way, step),
                grads.at[p, ring(three, 2), ring(two, step), :, half(way, 64)],
                first_rows.at[p, SIDE[way], SLOT[step]],
                neighbours[ORDER[p][2], way],
            )

    def add_first(p, way, step):
        one, two, three = places(p)
        arrived(("s1", p, way, step))
        ref = grads.at[p, ring(three, way), ring(two, step), :, half(way, 64)]
        ref[...] = (ref[...].astype(f32) + first_rows[p, SIDE[way], SLOT[step]].astype(f32)).astype(bf16)

    def send_row(p, step):
        one, two, three = places(p)
        for way in WAYS:
            add_first(p, way, step)
            send(
                ("s2", p, way, step),
                grads.at[p, ring(three, way), ring(two, step)],
                full_rows.at[p, SIDE[way], SLOT[step]],
                neighbours[ORDER[p][2], way],
            )

    def send_own_row(p, step):
        one, two, three = places(p)
        for way in WAYS:
            if ("added", p, way) not in seen:
                seen.add(("added", p, way))
                add_first(p, way, 0)
            send(
                ("s2u", p, way, step),
                grads.at[p, ring(three, way), two, ring(one, step)],
                full_units.at[p, SIDE[way], SLOT[step]],
                neighbours[ORDER[p][2], way],
            )

    def sum_row(p, step):
        one, two, three = places(p)
        arrived(*[("s2", p, way, step) for way in WAYS])
        return (
            grads[p, three, ring(two, step)].astype(f32)
            + full_rows[p, 0, SLOT[step]].astype(f32)
            + full_rows[p, 1, SLOT[step]].astype(f32)
        )

    def send_second(p):
        one, two, three = places(p)
        grads[p, three, ring(two, 2)] = sum_row(p, 2).astype(bf16)
        for way in WAYS:
            send(
                ("s3", p, way),
                grads.at[p, three, ring(two, 2), :, half(way, 64)],
                first_second.at[p, SIDE[way]],
                neighbours[ORDER[p][1], way],
            )

    def add_second(p):
        one, two, three = places(p)
        for way in WAYS:
            row = sum_row(p, way)
            arrived(("s3", p, way))
            low, high = row[:, :32], row[:, 32:]
            extra = first_second[p, SIDE[way]].astype(f32)
            low, high = (low + extra, high) if way == 1 else (low, high + extra)
            grads[p, three, ring(two, way), :, :32] = low.astype(bf16)
            grads[p, three, ring(two, way), :, 32:] = high.astype(bf16)

    def send_unit(p, step):
        one, two, three = places(p)
        for way in WAYS:
            send(
                ("s4", p, way, step),
                grads.at[p, three, ring(two, way), ring(one, step)],
                second_units.at[p, SIDE[way], SLOT[step]],
                neighbours[ORDER[p][1], way],
            )

    def sum_unit(p, step):
        one, two, three = places(p)
        total = grads[p, three, two, ring(one, step)].astype(f32)
        for way in WAYS:
            arrived(("s2u", p, way, step))
            total += full_units[p, SIDE[way], SLOT[step]].astype(f32)
        for way in WAYS:
            arrived(("s4", p, way, step))
            total += second_units[p, SIDE[way], SLOT[step]].astype(f32)
        return total

    def send_third(p):
        one, two, three = places(p)
        grads[p, three, two, ring(one, 2)] = sum_unit(p, 2).astype(bf16)
        for way in WAYS:
            send(
                ("s5", p, way),
                grads.at[p, three, two, ring(one, 2), half(way, 64)],
                first_last.at[p, SIDE[way]],
                neighbours[ORDER[p][0], way],
            )

    def send_last(p):
        one, two, three = places(p)
        for way in WAYS:
            total = sum_unit(p, way)
            arrived(("s5", p, way))
            low, high = total[:32], total[32:]
            extra = first_last[p, SIDE[way]].astype(f32)
            low, high = (low + extra, high) if way == 1 else (low, high + extra)
            grads[p, three, two, ring(one, way), :32] = low.astype(bf16)
            grads[p, three, two, ring(one, way), 32:] = high.astype(bf16)
            send(
                ("s6", p, way),
                grads.at[p, three, two, ring(one, way)],
                last_unit.at[p, SIDE[way]],
                neighbours[ORDER[p][0], way],
            )

    def finish(p):
        total = sum_unit(p, 0)
        for way in WAYS:
            arrived(("s6", p, way))
            total += last_unit[p, SIDE[way]].astype(f32)
        final[p * 64 : p * 64 + 64] = total

    actions = {
        "terms": terms, "first": send_first, "row": send_row, "own": send_own_row, "second": send_second,
        "add": add_second, "unit": send_unit, "third": send_third, "last": send_last, "end": finish,
    }
    for name, *rest in SCATTER:
        actions[name](*rest)

    def rows_of(which):
        return pl.ds(pl.multiple_of(which * 96, 96), 96)

    send(("end", 0), final.at[rows_of(1 - core)], finals, sibling)
    mine_sum = final[rows_of(core)]
    arrived(("end", 0))
    gradient_out[0, :, :256] = jnp.where(core == 0, mine_sum, finals[...])
    gradient_out[0, :, 256:] = jnp.where(core == 0, finals[...], mine_sum)

    for index, *view in leaving.values():
        if view:
            pltpu.make_async_copy(view[0], view[0], send_sems.at[index]).wait()


def per_device(params, moment, second, grad_prev, tokens, cotangent):
    shard = (1, 96, 512)
    gradient = pl.pallas_call(
        kernel,
        out_shape=pltpu.VMEM(shard, f32),
        in_specs=[pl.BlockSpec(memory_space=pl.ANY)] * 6,
        out_specs=pl.BlockSpec(memory_space=pltpu.VMEM),
        scratch_shapes=[
            pltpu.VMEM((768, 12288), bf16),
            pltpu.VMEM((3, 4, 4, 4, 64, 256), bf16),
            pltpu.VMEM((3, 4, 4, 4, 64, 256), bf16),
            pltpu.VMEM((768, 256), f32),
            pltpu.VMEM((768, 256), f32),
            pltpu.VMEM((768, 256), bf16),
            pltpu.VMEM((3, 96, 256), bf16),
            pltpu.VMEM((96, 512), bf16),
            pltpu.VMEM((96, 512), bf16),
            pltpu.VMEM((96, 512), bf16),
            pltpu.VMEM((96, 512), f32),
            pltpu.VMEM((3, 2, 4, 4, 32, 256), bf16),
            pltpu.VMEM((3, 2, 3, 4, 64, 256), bf16),
            pltpu.VMEM((3, 2, 4, 64, 256), bf16),
            pltpu.VMEM((3, 2, 4, 32, 256), bf16),
            pltpu.VMEM((3, 2, 4, 64, 256), bf16),
            pltpu.VMEM((3, 2, 32, 256), bf16),
            pltpu.VMEM((3, 2, 64, 256), bf16),
            pltpu.VMEM((192, 256), f32),
            pltpu.VMEM((96, 256), f32),
            pltpu.SemaphoreType.DMA((9,)),
            pltpu.SemaphoreType.DMA((95,)),
            pltpu.SemaphoreType.DMA((7,)),
        ],
        compiler_params=pltpu.CompilerParams(
            collective_id=0, has_side_effects=True, vmem_limit_bytes=56 * 2**20
        ),
    )(params, moment, second, grad_prev, tokens, cotangent)
    return adam_update(params, moment, second, grad_prev) + (gradient,)


def solution(mesh):
    blocks = P("inner", "outer", None)
    rows = P(("outer", "inner"), None)
    return jax.shard_map(
        per_device,
        mesh=mesh,
        in_specs=(blocks,) * 4 + (rows,) * 2,
        out_specs=(blocks,) * 4,
        check_vma=False,
    )
```

```python
import functools

import jax
import jax.numpy as jnp
from jax import lax
from jax.experimental import pallas as pl
from jax.experimental.pallas import tpu as pltpu
from jax.sharding import PartitionSpec as P

beta_one = 0.9
beta_two = 0.95
bias_one = 0.9999734386011124
bias_two = 0.994079470779666
epsilon_adam = 1e-08
learn_rate = 6e-05
decay_rate = 0.1
root_scale = 0.7978845608028654
cubic_term = 0.044715

MESH = pl.DeviceIdType.MESH
f32 = jnp.float32
bf16 = jnp.bfloat16

ORDER = ((0, 1, 2), (1, 2, 0), (2, 0, 1))
STEPS = (2, 1, -1, 0)
SLOT = {2: 0, 1: 1, -1: 2, 0: 3}
WAYS = (1, -1)
SIDE = {1: 0, -1: 1}


def gelu_value(values):
    tangent = jnp.tanh(root_scale * (values + cubic_term * values * values * values))
    return 0.5 * values * (1.0 + tangent)


def gelu_slope(values):
    tangent = jnp.tanh(root_scale * (values + cubic_term * values * values * values))
    return 0.5 * (1.0 + tangent) + 0.5 * values * (1.0 - tangent * tangent) * root_scale * (
        1.0 + 3.0 * cubic_term * values * values
    )


def adam_update(params, moment, second, grad_prev):
    moment_new = beta_one * moment.astype(f32) + (1.0 - beta_one) * grad_prev
    second_new = beta_two * second.astype(f32) + (1.0 - beta_two) * grad_prev * grad_prev
    update = moment_new / bias_one / (
        jnp.sqrt(second_new / bias_two) + epsilon_adam
    ) + decay_rate * params.astype(f32)
    fresh = params.astype(f32) - learn_rate * update
    return (fresh.astype(bf16), moment_new.astype(bf16), second_new.astype(bf16))


def ring(place, step):
    return lax.rem(place + (step + 4), 4)


def device(x, y, z, core):
    return {"outer": z * 4 + lax.rem(y, 2) * 2 + core, "inner": x * 2 + y // 2}


GATHER = (
    ("own", 1, 0), ("own", 0, 0), ("own", 2, 0), ("own", 2, 2), ("own", 0, 2), ("own", 1, 1), ("own", 2, 1),
    ("own", 1, 2), ("own", 0, 1), ("unit", 0, 1, -1), ("unit", 1, 1, -1), ("unit", 0, 1, 1), ("unit", 2, 1, 1),
    ("unit", 2, 2, -1), ("unit", 2, 1, -1), ("unit", 0, 2, 1), ("unit", 1, 2, 1), ("second", 2, 0), ("unit", 1, 1, 1),
    ("unit", 1, 1, 2), ("unit", 0, 1, 2), ("unit", 2, 2, 1), ("unit", 2, 1, 2), ("unit", 0, 2, 2), ("unit", 2, 2, 2),
    ("second", 0, -1), ("unit", 1, 2, -1), ("second", 0, 0), ("second", 1, -1), ("unit", 0, 2, -1), ("second", 0, 1),
    ("second", 1, 0), ("second", 2, 1), ("second", 2, -1), ("second", 1, 1), ("unit", 1, 2, 2), ("second", 1, 2),
    ("row", 1, -1), ("second", 0, 2), ("row", 0, -1), ("row", 2, -1), ("row", 2, 1), ("row", 0, 1), ("second", 2, 2),
    ("row", 1, 1), ("third", 1, 0), ("row", 1, 2), ("row", 2, 2), ("row", 0, 2), ("third", 2, 0), ("third", 0, 0),
    ("mul", 0), ("third", 1, 1), ("third", 2, 1), ("third", 0, 1), ("mul", 2), ("third", 0, -1), ("third", 1, -1),
    ("third", 2, -1), ("mul", 1), ("mul", 3), ("third", 0, 2), ("third", 2, 2), ("third", 1, 2), ("mul", 4),
    ("mul", 5), ("mul", 6), ("mul", 7),
)
SCATTER = (
    ("terms", 0), ("first", 1, 2), ("terms", 1), ("first", 2, 2), ("terms", 2), ("first", 0, -1), ("row", 1, 2),
    ("terms", 3), ("first", 0, 1), ("first", 2, 1), ("first", 0, 2), ("first", 1, -1), ("row", 2, 2), ("first", 0, 0),
    ("terms", 5), ("first", 1, 1), ("first", 1, 0), ("first", 2, 0), ("second", 1), ("terms", 4), ("first", 2, -1),
    ("row", 0, 2), ("row", 1, -1), ("row", 2, 1), ("row", 1, 1), ("row", 0, 1), ("row", 0, -1), ("row", 2, -1),
    ("second", 0), ("second", 2), ("own", 1, 1), ("own", 0, 1), ("own", 2, -1), ("own", 0, -1), ("own", 2, 2),
    ("add", 1), ("own", 1, 2), ("own", 1, -1), ("own", 2, 1), ("add", 2), ("unit", 1, 1), ("unit", 2, -1),
    ("unit", 1, 2), ("unit", 2, 2), ("unit", 2, 1), ("unit", 1, -1), ("add", 0), ("unit", 0, 1), ("unit", 0, 2),
    ("own", 1, 0), ("own", 0, 2), ("unit", 0, -1), ("unit", 2, 0), ("unit", 1, 0), ("unit", 0, 0), ("last", 1),
    ("last", 2), ("own", 0, 0), ("last", 0), ("own", 2, 0), ("end", 1), ("end", 2), ("end", 0),
)


def kernel(
    params, moment, second, grad_prev, tokens, cotangent,
    gradient_out,
    act, held, grads, acc, other, factor, stage,
    old_params, old_moment, old_second, old_grad,
    first_rows, full_rows, full_units, first_second, second_units, last_units,
    final, finals, send_sems, recv_sems, local_sems,
):
    outer = lax.axis_index("outer")
    inner = lax.axis_index("inner")
    core = lax.rem(outer, 2)
    y_lo = lax.rem(outer // 2, 2)
    y_hi = lax.rem(inner, 2)
    own = (inner // 2, y_hi * 2 + y_lo, outer // 4)

    def neighbour(axis, way):
        place = list(own)
        place[axis] = ring(place[axis], way)
        return device(*place, core)

    neighbours = {(axis, way): neighbour(axis, way) for axis in range(3) for way in (1, -1, 2)}
    sibling = device(*own, 1 - core)

    barrier = pltpu.get_barrier_semaphore()
    greeted = list(neighbours.values()) + [sibling]
    for one in greeted:
        pl.semaphore_signal(barrier, inc=1, device_id=one, device_id_type=MESH)

    old = [
        pltpu.make_async_copy(source.at[0], target, local_sems.at[3 + index])
        for index, (source, target) in enumerate(
            ((params, old_params), (moment, old_moment), (second, old_second), (grad_prev, old_grad))
        )
    ]
    for copy in old:
        copy.start()

    mine = pl.ds(pl.multiple_of(core * 384, 384), 384)

    def load_own(source):
        return pltpu.make_async_copy(source, act.at[mine], local_sems.at[0])

    @pl.when(core == 0)
    def _():
        load_own(tokens).start()

    @pl.when(core == 1)
    def _():
        load_own(cotangent).start()

    groups = {}
    seen = set()
    leaving = {
        "rows": (0, stage.at[0]),
        "g1": (1, held.at[:, 0, 0, 0:3]), "g2": (2, held.at[:, 0, 0:3]), "g2f": (2,),
        "g3": (3, held.at[:, 0:3]), "g3r": (3,), "g3f": (3,),
        "products": (4, acc),
        "s1": (5, grads.at[:, 0:3]), "s2": (5,), "s2u": (5,), "s3": (6, grads.at[:, 0, 0:3]), "s4": (6,),
        "s6": (7, grads.at[:, 0, 0, 0:3]),
        "end": (8, finals),
    }

    def coming(key):
        name, p = key[0], key[1]
        if name in ("rows", "end"):
            return (name,), stage.at[2] if name == "rows" else finals
        if name == "products":
            return key, other.at[0:384]
        if name == "g3f":
            return (name, key[3]), held.at[:, 0, 0]
        ref = held if name[0] == "g" else grads
        if name in ("g1", "s6"):
            return (name, p), ref.at[p, 0, 0, 0:3]
        if name in ("g2f", "s3"):
            return (name, p), ref.at[p, 0, 0]
        if name == "g3":
            return (name, p), ref.at[p, 0, 0:2]
        if name in ("g2", "s2u", "s4"):
            return (name, p, key[3]), ref.at[p, 0, 0, 0:2]
        if name == "s1":
            return (name, p, key[3]), ref.at[p, 0, 0]
        return (name, p, key[3]), ref.at[p, 0, 0:2]

    def send(key, source, target, to):
        group = coming(key)[0]
        index = groups.setdefault(group, len(groups))
        pltpu.make_async_remote_copy(
            src_ref=source,
            dst_ref=target,
            send_sem=send_sems.at[leaving[key[0]][0]],
            recv_sem=recv_sems.at[index],
            device_id=to,
            device_id_type=MESH,
        ).start()

    def arrived(*keys):
        for key in keys:
            group, view = coming(key)
            if group not in seen:
                seen.add(group)
                pltpu.make_async_copy(view, view, recv_sems.at[groups[group]]).wait()

    for copy in old:
        copy.wait()

    def fresh(columns):
        return adam_update(
            old_params[:, columns], old_moment[:, columns], old_second[:, columns], old_grad[:, columns]
        )[0]

    stage[0] = fresh(slice(0, 256))
    stage[1] = fresh(slice(256, 512))

    pl.semaphore_wait(barrier, len(greeted))

    send(("rows", 0), stage.at[1 - core], stage.at[2], sibling)

    def load_sibling(source):
        return pltpu.make_async_remote_copy(
            src_ref=source,
            dst_ref=act.at[mine],
            send_sem=local_sems.at[1],
            recv_sem=local_sems.at[2],
            device_id=sibling,
            device_id_type=MESH,
        )

    @pl.when(core == 0)
    def _():
        load_sibling(cotangent).start()

    @pl.when(core == 1)
    def _():
        load_sibling(tokens).start()

    def places(p):
        return tuple(own[axis] for axis in ORDER[p])

    arrived(("rows", 0))
    for first_core in range(2):
        @pl.when(core == first_core)
        def _():
            low, high = (stage[first_core], stage[2]) if first_core == 0 else (stage[2], stage[first_core])
            pieces = (low[:64], jnp.concatenate([low[64:], high[:32]], axis=0), high[32:])
            for p in range(3):
                one, two, three = places(p)
                held[p, three, two, one] = pieces[p]

    def half(way, rows):
        return pl.ds(SIDE[way] * (rows // 2), rows // 2)

    def unit(p, three, two, one):
        return held.at[p, three, two, one]

    def give(key, p, level, ref):
        for way in WAYS:
            send((key[0], p, way) + key[1:], ref, ref, neighbours[ORDER[p][level], way])

    def pass_on(key, p, level, way, ref):
        send(key, ref, ref, neighbours[ORDER[p][level], way])

    def give_own(p, level):
        one, two, three = places(p)
        ref = unit(p, three, two, one)
        if level:
            give((f"g{level + 1}", 0), p, level, ref)
            return
        for step in (2, 1, -1):
            send(("g1", p, step), ref, ref, neighbours[ORDER[p][0], step])

    def give_unit(p, level, step):
        one, two, three = places(p)
        arrived(("g1", p, step))
        give((f"g{level + 1}", step), p, level, unit(p, three, two, ring(one, step)))

    def pass_second(p, step):
        one, two, three = places(p)
        for way in WAYS:
            arrived(("g2", p, way, step))
            pass_on(
                ("g2f", p, way, step), p, 1, way,
                held.at[p, three, ring(two, -way), ring(one, step), half(way, 64)],
            )

    def give_row(p, step):
        one, two, three = places(p)
        if step == 2:
            arrived(*[("g2f", p, way, k) for way in WAYS for k in STEPS])
        else:
            arrived(*[("g2", p, -step, k) for k in STEPS])
        give(("g3r", step), p, 2, held.at[p, three, ring(two, step)])

    def third(p, way, step):
        return [("g3", p, way, k) for k in STEPS] if step == 0 else [("g3r", p, way, step)]

    def pass_third(p, step):
        one, two, three = places(p)
        for way in WAYS:
            arrived(*third(p, way, step))
            pass_on(
                ("g3f", p, way, step), p, 2, way,
                held.at[p, ring(three, -way), ring(two, step), :, half(way, 64)],
            )

    def block(p, x, y, z):
        place = (x, y, z)
        return tuple(place[axis] for axis in reversed(ORDER[p]))

    def columns(x, part, z):
        return pl.ds(pl.multiple_of(x * 3072 + part * 1536 + z * 384, 128), 384)

    def chunk_product(chunks, rows=slice(None)):
        left, right = [], []
        for step_x, flip, step_z in chunks:
            x, part, z = ring(own[0], step_x), lax.rem(y_hi + flip, 2), ring(own[2], step_z)
            left.append(act[rows, columns(x, part, z)])
            right += [held[(p,) + block(p, x, part * 2 + low, z)] for low in range(2) for p in range(3)]
        return jnp.dot(
            jnp.concatenate(left, axis=1), jnp.concatenate(right, axis=0), preferred_element_type=f32
        )

    near = (0, 1, -1)

    def multiply(which):
        if "loaded" not in seen:
            seen.add("loaded")
            load_own(tokens).wait()
            load_sibling(tokens).wait()
        for p in range(3):
            arrived(("g1", p, 1), *[("g2", p, 1, k) for k in STEPS])
            if which >= 3:
                arrived(("g2f", p, 1, 0))
            for way in WAYS:
                for step in near:
                    arrived(*third(p, way, step))
                if which >= 3:
                    arrived(*third(p, way, 2))
                    for step in near[: which - 2]:
                        arrived(("g3f", p, way, step))
        if which < 3:
            todo = [(near[which], 0, z) for z in near]
        elif which < 6:
            todo = [(near[which - 3], 1, z) for z in near]
        elif which == 6:
            todo = [(2, 0, z) for z in near]
        else:
            todo = [(x, 0, 2) for x in near]
        part = chunk_product(todo)
        if which:
            acc[...] += part
        else:
            acc[...] = part

    actions = {
        "own": give_own, "unit": give_unit, "second": pass_second,
        "row": give_row, "third": pass_third, "mul": multiply,
    }
    for name, *rest in GATHER:
        actions[name](*rest)
    for p in range(3):
        for way in WAYS:
            arrived(("g3f", p, way, 2))
    last = [(2, 0, 2)] + [(2, 1, z) for z in (0, 1, -1, 2)] + [(x, 1, 2) for x in near]
    for index in range(2):
        rows = slice(index * 384, index * 384 + 384)
        acc[rows] += chunk_product(last, rows)
        send(("products", index), acc.at[rows], other.at[rows], sibling)
    for index in range(2):
        arrived(("products", index))
        for start in range(index * 384, index * 384 + 384, 128):
            span = slice(start, start + 128)

            @pl.when(core == 0)
            def _():
                factor[span] = (other[span] * gelu_slope(acc[span])).astype(bf16)

            @pl.when(core == 1)
            def _():
                factor[span] = gelu_value(other[span]).astype(bf16)

    def term(x, z):
        for part in range(2):
            result = lax.dot_general(
                act[:, columns(x, part, z)], factor[...], (((0,), (0,)), ((), ())), preferred_element_type=f32
            ).astype(bf16)
            for low in range(2):
                for p in range(3):
                    start = (low * 3 + p) * 64
                    grads[(p,) + block(p, x, part * 2 + low, z)] = result[start : start + 64]

    def terms(which):
        x, z = own[0], own[2]
        if which == 0:
            term(ring(x, 2), ring(z, 2))
            return

        def body(index, carry):
            step = index - 1
            if which < 2:
                term(ring(x, 2), ring(z, step))
            elif which == 2:
                term(ring(x, step), ring(z, 2))
            else:
                term(ring(x, (1, -1, 0)[which - 3]), ring(z, step))
            return carry

        lax.fori_loop(0, 3, body, 0)

    def send_first(p, step):
        one, two, three = places(p)
        for way in WAYS:
            send(
                ("s1", p, way, step),
                grads.at[p, ring(three, 2), ring(two, step), :, half(way, 64)],
                first_rows.at[p, SIDE[way], SLOT[step]],
                neighbours[ORDER[p][2], way],
            )

    def add_first(p, way, step):
        one, two, three = places(p)
        arrived(("s1", p, way, step))
        ref = grads.at[p, ring(three, way), ring(two, step), :, half(way, 64)]
        ref[...] = (ref[...].astype(f32) + first_rows[p, SIDE[way], SLOT[step]].astype(f32)).astype(bf16)

    def send_row(p, step):
        one, two, three = places(p)
        for way in WAYS:
            add_first(p, way, step)
            send(
                ("s2", p, way, step),
                grads.at[p, ring(three, way), ring(two, step)],
                full_rows.at[p, SIDE[way], SLOT[step]],
                neighbours[ORDER[p][2], way],
            )

    def send_own_row(p, step):
        one, two, three = places(p)
        for way in WAYS:
            if ("added", p, way) not in seen:
                seen.add(("added", p, way))
                add_first(p, way, 0)
            send(
                ("s2u", p, way, step),
                grads.at[p, ring(three, way), two, ring(one, step)],
                full_units.at[p, SIDE[way], SLOT[step]],
                neighbours[ORDER[p][2], way],
            )

    def sum_row(p, step):
        one, two, three = places(p)
        arrived(*[("s2", p, way, step) for way in WAYS])
        return (
            grads[p, three, ring(two, step)].astype(f32)
            + full_rows[p, 0, SLOT[step]].astype(f32)
            + full_rows[p, 1, SLOT[step]].astype(f32)
        )

    def send_second(p):
        one, two, three = places(p)
        grads[p, three, ring(two, 2)] = sum_row(p, 2).astype(bf16)
        for way in WAYS:
            send(
                ("s3", p, way),
                grads.at[p, three, ring(two, 2), :, half(way, 64)],
                first_second.at[p, SIDE[way]],
                neighbours[ORDER[p][1], way],
            )

    def add_second(p):
        one, two, three = places(p)
        for way in WAYS:
            row = sum_row(p, way)
            arrived(("s3", p, way))
            low, high = row[:, :32], row[:, 32:]
            extra = first_second[p, SIDE[way]].astype(f32)
            low, high = (low + extra, high) if way == 1 else (low, high + extra)
            grads[p, three, ring(two, way), :, :32] = low.astype(bf16)
            grads[p, three, ring(two, way), :, 32:] = high.astype(bf16)

    def send_unit(p, step):
        one, two, three = places(p)
        for way in WAYS:
            send(
                ("s4", p, way, step),
                grads.at[p, three, ring(two, way), ring(one, step)],
                second_units.at[p, SIDE[way], SLOT[step]],
                neighbours[ORDER[p][1], way],
            )

    def sum_unit(p, step):
        one, two, three = places(p)
        total = grads[p, three, two, ring(one, step)].astype(f32)
        for way in WAYS:
            arrived(("s2u", p, way, step))
            total += full_units[p, SIDE[way], SLOT[step]].astype(f32)
        for way in WAYS:
            arrived(("s4", p, way, step))
            total += second_units[p, SIDE[way], SLOT[step]].astype(f32)
        return total

    def send_last(p):
        one, two, three = places(p)
        for step in (2, 1, -1):
            grads[p, three, two, ring(one, step)] = sum_unit(p, step).astype(bf16)
            send(
                ("s6", p, step),
                grads.at[p, three, two, ring(one, step)],
                last_units.at[p, SLOT[step]],
                neighbours[ORDER[p][0], step],
            )

    def finish(p):
        total = sum_unit(p, 0)
        arrived(("s6", p, 2))
        for step in (2, 1, -1):
            total += last_units[p, SLOT[step]].astype(f32)
        final[p * 64 : p * 64 + 64] = total

    actions = {
        "terms": terms, "first": send_first, "row": send_row, "own": send_own_row, "second": send_second,
        "add": add_second, "unit": send_unit, "last": send_last, "end": finish,
    }
    for name, *rest in SCATTER:
        actions[name](*rest)

    def rows_of(which):
        return pl.ds(pl.multiple_of(which * 96, 96), 96)

    send(("end", 0), final.at[rows_of(1 - core)], finals, sibling)
    mine_sum = final[rows_of(core)]
    arrived(("end", 0))
    gradient_out[0, :, :256] = jnp.where(core == 0, mine_sum, finals[...])
    gradient_out[0, :, 256:] = jnp.where(core == 0, finals[...], mine_sum)

    for index, *view in leaving.values():
        if view:
            pltpu.make_async_copy(view[0], view[0], send_sems.at[index]).wait()


def per_device(params, moment, second, grad_prev, tokens, cotangent):
    shard = (1, 96, 512)
    gradient = pl.pallas_call(
        kernel,
        out_shape=pltpu.VMEM(shard, f32),
        in_specs=[pl.BlockSpec(memory_space=pl.ANY)] * 6,
        out_specs=pl.BlockSpec(memory_space=pltpu.VMEM),
        scratch_shapes=[
            pltpu.VMEM((768, 12288), bf16),
            pltpu.VMEM((3, 4, 4, 4, 64, 256), bf16),
            pltpu.VMEM((3, 4, 4, 4, 64, 256), bf16),
            pltpu.VMEM((768, 256), f32),
            pltpu.VMEM((768, 256), f32),
            pltpu.VMEM((768, 256), bf16),
            pltpu.VMEM((3, 96, 256), bf16),
            pltpu.VMEM((96, 512), bf16),
            pltpu.VMEM((96, 512), bf16),
            pltpu.VMEM((96, 512), bf16),
            pltpu.VMEM((96, 512), f32),
            pltpu.VMEM((3, 2, 4, 4, 32, 256), bf16),
            pltpu.VMEM((3, 2, 3, 4, 64, 256), bf16),
            pltpu.VMEM((3, 2, 4, 64, 256), bf16),
            pltpu.VMEM((3, 2, 4, 32, 256), bf16),
            pltpu.VMEM((3, 2, 4, 64, 256), bf16),
            pltpu.VMEM((3, 3, 64, 256), bf16),
            pltpu.VMEM((192, 256), f32),
            pltpu.VMEM((96, 256), f32),
            pltpu.SemaphoreType.DMA((9,)),
            pltpu.SemaphoreType.DMA((89,)),
            pltpu.SemaphoreType.DMA((7,)),
        ],
        compiler_params=pltpu.CompilerParams(
            collective_id=0, has_side_effects=True, vmem_limit_bytes=56 * 2**20
        ),
    )(params, moment, second, grad_prev, tokens, cotangent)
    return adam_update(params, moment, second, grad_prev) + (gradient,)


def solution(mesh):
    blocks = P("inner", "outer", None)
    rows = P(("outer", "inner"), None)
    return jax.shard_map(
        per_device,
        mesh=mesh,
        in_specs=(blocks,) * 4 + (rows,) * 2,
        out_specs=(blocks,) * 4,
        check_vma=False,
    )
```
